32 devices in a mesh: row: 4 (over y, x), col: 8 (over z, core).
Axes of the slice: x: 2, y: 2, z: 4, core: 2. Of those that a mesh axis runs over, the one named last changes fastest.
Arguments:
- ainv_top: float32 [4096, 4096], P('row', 'col'), may hold values from -6 to 6
- block_owner: int32 [32], replicated, may hold values from 0 to 31, as said below
- upper_list: int32 [16, 16], P('col'), may hold values from 0 to 31, as said below
- upper_len: int32 [16], P('col'), may hold values from 12 to 16
- upper_panel: float32 [16, 2048, 128], P('col', 'row'), may hold values from -0.125 to 0.125
- upper_dinv: float32 [16, 128, 128], P('col'), may hold values from -6 to 6
- lower_len: int32 [16], P('col'), may hold values from 8 to 16, as said below
- lower_panel: float32 [16, 2048, 128], P('col', 'row'), may hold values from -0.125 to 0.125
- lower_parent: float32 [16, 128, 128], P('col'), may hold values from -0.5 to 0.5
- lower_dinv: float32 [16, 128, 128], P('col'), may hold values from -6 to 6
Outputs:
- upper_offdiag: float32 [16, 128, 4096], P('col', None, 'row')
- upper_diag: float32 [16, 128, 128], P('col')
- lower_offdiag: float32 [16, 128, 4096], P('col', None, 'row')
- lower_parent_block: float32 [16, 128, 128], P('col')
- lower_diag: float32 [16, 128, 128], P('col')
The draws below stay inside these ranges and needn't reach their ends.
Inputs may be any that keep to these rules, and one draw needn't show every extreme that they name: `block_owner`: a permutation of the storage blocks. `upper_list`: each row holds 16 different logical top block indices; their storage blocks are exactly 2 of each run of 4 storage blocks that starts at a multiple of 4. `lower_len`: never more than upper_len of the same supernode.
All inputs are finite; a program needn't handle non-finite values.
Results may differ from the reference program's by a relative error of at most 0.0003.
Values sent between devices are 32-bit elements; how exact they have to be, the bound alone decides.
A program may use at most 192 MiB of HBM per device.

```python
import jax
import jax.numpy as jnp
from jax import lax

B = 128
TOP_COLS = 4
NT = 32
P_SIZE = 16
SUPER = 16


def lengths_pair(key):
    base = jax.random.fold_in(key, 11)
    first_key, second_key = jax.random.split(base)
    upper = jax.random.randint(first_key, (SUPER,), P_SIZE - P_SIZE // 4, P_SIZE + 1)
    upper = upper.at[0].set(P_SIZE).at[1].set(P_SIZE - P_SIZE // 4)
    scaled = jax.random.randint(second_key, (SUPER,), 0, 1 << 20)
    lower = P_SIZE // 2 + scaled * (upper - P_SIZE // 2 + 1) // (1 << 20)
    lower = lower.at[0].set(P_SIZE).at[1].set(P_SIZE // 2)
    return (upper.astype(jnp.int32), lower.astype(jnp.int32))


def storage_plan(key):
    owner = jax.random.permutation(jax.random.fold_in(key, 3), NT).astype(jnp.int32)
    groups = NT // TOP_COLS
    pick_keys = jax.random.split(jax.random.fold_in(key, 5), SUPER * groups)
    picks = jax.vmap(lambda one_key: jax.random.permutation(one_key, TOP_COLS))(pick_keys)[:, :TOP_COLS // 2]
    picks = picks.reshape(SUPER, groups, TOP_COLS // 2) + (jnp.arange(groups, dtype=jnp.int32) * TOP_COLS)[None, :, None]
    slots = picks.reshape(SUPER, P_SIZE).astype(jnp.int32)
    order_keys = jax.random.split(jax.random.fold_in(key, 9), SUPER)
    shuffles = jax.vmap(lambda one_key: jax.random.permutation(one_key, P_SIZE))(order_keys)
    slots = jnp.take_along_axis(slots, shuffles, axis=1)
    inverse = jnp.zeros((NT,), jnp.int32).at[owner].set(jnp.arange(NT, dtype=jnp.int32))
    return (owner, inverse[slots].astype(jnp.int32))


def draw_block_owner(key, part):
    return storage_plan(key)[0]


def draw_upper_list(key, part):
    return storage_plan(key)[1]


def draw_upper_len(key, part):
    return lengths_pair(key)[0]


def draw_lower_len(key, part):
    return lengths_pair(key)[1]


def level_of(key, shape, cuts, low, top_value):
    level = 1.0
    for axis_at, blocks in cuts:
        draws = jax.random.uniform(jax.random.fold_in(jax.random.fold_in(key, 6), axis_at), (blocks,), jnp.float32, low / len(cuts), top_value / len(cuts))
        level = level * jnp.repeat(jnp.exp(draws), shape[axis_at] // blocks).reshape((-1,) + (1,) * (len(shape) - 1 - axis_at))
    return level


def bell_draw(own_key, dims, width, limit, cuts=(), kind=jnp.bfloat16):
    gain = level_of(own_key, dims, cuts, -0.22, 0.18) if cuts else 1.0
    entries = jax.random.normal(own_key, dims, jnp.float32) * width * gain
    return jnp.minimum(jnp.maximum(entries, -limit), limit).astype(kind)


def setup_inputs(seed: int = 0) -> dict:
    arg_keys = jax.random.split(jax.random.key(seed), 11)
    return {
        "ainv_top": bell_draw(arg_keys[0], (NT * B, NT * B), 1.0, 6.0, ((0, 4), (1, 8)), jnp.float32),
        "block_owner": draw_block_owner(jax.random.fold_in(arg_keys[10], 71), 0),
        "upper_list": draw_upper_list(jax.random.fold_in(arg_keys[10], 71), 0),
        "upper_len": draw_upper_len(jax.random.fold_in(arg_keys[10], 71), 0),
        "upper_panel": bell_draw(arg_keys[4], (SUPER, P_SIZE * B, B), (P_SIZE * B) ** -0.5, 0.125, ((0, 8), (1, 4)), jnp.float32),
        "upper_dinv": bell_draw(arg_keys[5], (SUPER, B, B), 1.0, 6.0, ((0, 8),), jnp.float32),
        "lower_len": draw_lower_len(jax.random.fold_in(arg_keys[10], 71), 0),
        "lower_panel": bell_draw(arg_keys[7], (SUPER, P_SIZE * B, B), (P_SIZE * B) ** -0.5, 0.125, ((0, 8), (1, 4)), jnp.float32),
        "lower_parent": bell_draw(arg_keys[8], (SUPER, B, B), B ** -0.5, 0.5, ((0, 8),), jnp.float32),
        "lower_dinv": bell_draw(arg_keys[9], (SUPER, B, B), 1.0, 6.0, ((0, 8),), jnp.float32),
    }


highest = lax.Precision.HIGHEST


def matmul(left, right):
    return jnp.dot(left, right, precision=highest, preferred_element_type=jnp.float32)


def reference(ainv_top, block_owner, upper_list, upper_len, upper_panel, upper_dinv, lower_len, lower_panel, lower_parent, lower_dinv):
    block_w = upper_dinv.shape[-1]
    inside = jnp.arange(block_w, dtype=jnp.int32)
    places = jnp.arange(upper_list.shape[1], dtype=jnp.int32)
    total_cols = ainv_top.shape[1]

    def one_node(items):
        names, upper_count, upper_full, upper_inv, lower_count, lower_full, parent_block, lower_inv = items
        slots = block_owner[names].astype(jnp.int32)
        rows = (slots[:, None] * block_w + inside[None, :]).reshape(-1)
        chosen = jnp.take(jnp.take(ainv_top, rows, axis=0), rows, axis=1)
        keep_up = jnp.repeat((places < upper_count).astype(jnp.float32), block_w)[:, None]
        keep_low = jnp.repeat((places < lower_count).astype(jnp.float32), block_w)[:, None]
        panel_up = upper_full * keep_up
        panel_low = lower_full * keep_low
        g_up = -matmul(chosen, panel_up) * keep_up
        diag_up = upper_inv - matmul(panel_up.T, g_up)
        g_low = -(matmul(chosen, panel_low) + matmul(g_up, parent_block)) * keep_low
        parent_row = -(matmul(diag_up, parent_block) + matmul(g_up.T, panel_low))
        diag_low = lower_inv - matmul(parent_block.T, parent_row) - matmul(panel_low.T, g_low)
        off_up = jnp.zeros((block_w, total_cols), jnp.float32).at[:, rows].set(g_up.T)
        off_low = jnp.zeros((block_w, total_cols), jnp.float32).at[:, rows].set(g_low.T)
        return off_up, diag_up, off_low, parent_row, diag_low

    outputs = lax.map(one_node, (upper_list, upper_len, upper_panel, upper_dinv, lower_len, lower_panel, lower_parent, lower_dinv))
    return (outputs[0], outputs[1], outputs[2], outputs[3], outputs[4])
```

```python
import functools

import jax
import jax.numpy as jnp
from jax import lax
from jax.experimental import pallas as pl
from jax.experimental.pallas import tpu as pltpu
from jax.sharding import PartitionSpec as P

highest = lax.Precision.HIGHEST
VMEM = pltpu.VMEM
SMEM = pltpu.SMEM


def nt(left, right):
    return lax.dot_general(
        left, right, (((1,), (1,)), ((), ())), precision=highest, preferred_element_type=jnp.float32
    )


def tn(left, right):
    return lax.dot_general(
        left, right, (((0,), (0,)), ((), ())), precision=highest, preferred_element_type=jnp.float32
    )


def split_bf16(value):
    high = value.astype(jnp.bfloat16)
    low = (value - high.astype(jnp.float32)).astype(jnp.bfloat16)
    return high, low


def pick_kernel(order_ref, live_ref, panel_ref, out_ref):
    for place in range(out_ref.shape[0]):
        block = panel_ref[order_ref[place]]
        kept = jnp.where(live_ref[place] > 0, block, 0.0)
        out_ref[place] = kept.T


def product_kernel(per_col, row_ref, col_ref, ainv_ref, panel_ref, out_ref, high_ref, low_ref):
    col_blocks, row_blocks, width, _ = high_ref.shape
    step = pl.program_id(0)

    @pl.when(step == 0)
    def _():
        for cb in range(col_blocks):
            for rb in range(row_blocks):
                block = ainv_ref[rb * width:(rb + 1) * width, cb * width:(cb + 1) * width]
                high, low = split_bf16(block)
                high_ref[cb, rb] = high
                low_ref[cb, rb] = low

    n_row, _, col_live, piece, _ = panel_ref.shape
    row_live = out_ref.shape[3] // width
    parts = n_row // (2 * per_col)
    for node in range(per_col):
        rows = []
        for panel in range(2):
            for part in range(parts):
                source = (panel * per_col + node) * parts + part
                rows.append(jnp.concatenate([panel_ref[source, 0, s] for s in range(col_live)], axis=1))
        left = jnp.concatenate(rows, axis=0)
        left_high, left_low = split_bf16(left)
        left_all = jnp.concatenate([left_high, left_high, left_low], axis=1)
        at = step * per_col + node
        for rb in range(row_live):
            row = row_ref[at, rb]
            cols = [col_ref[at, s] for s in range(col_live)]
            high = [high_ref[cb, row] for cb in cols]
            low = [low_ref[cb, row] for cb in cols]
            right = jnp.concatenate(high + low + high, axis=1)
            total = lax.dot_general(
                left_all, right, (((1,), (1,)), ((), ())), preferred_element_type=jnp.float32
            )
            for panel in range(2):
                out_ref[0, panel * per_col + node, :, rb * width:(rb + 1) * width] = (
                    -total[panel * width:(panel + 1) * width]
                )


def finish_kernel(per_col, at_ref, up_ref, low_ref, sums_ref, local_ref, parent_ref,
                  up_off_ref, low_off_ref, terms_ref):
    width = parent_ref.shape[-1]
    n_row, count, piece, _ = local_ref.shape
    parts = n_row // (2 * per_col)
    up_off_ref[...] = jnp.zeros_like(up_off_ref)
    low_off_ref[...] = jnp.zeros_like(low_off_ref)

    def whole(combo, place):
        return jnp.concatenate([local_ref[combo * parts + part, place] for part in range(parts)], axis=0)

    for node in range(per_col):
        upper_term = jnp.zeros((width, width), jnp.float32)
        cross_term = jnp.zeros((width, width), jnp.float32)
        lower_term = jnp.zeros((width, width), jnp.float32)
        for place in range(count):
            span = slice(place * width, (place + 1) * width)
            upper = jnp.where(up_ref[node, place] > 0, sums_ref[node, :, span], 0.0)
            lower = sums_ref[per_col + node, :, span] - tn(parent_ref[node], upper)
            lower = jnp.where(low_ref[node, place] > 0, lower, 0.0)
            at = pl.ds(pl.multiple_of(at_ref[node, place] * width, width), width)
            up_off_ref[node, :, at] = upper
            low_off_ref[node, :, at] = lower
            local_up = whole(node, place)
            local_low = whole(per_col + node, place)
            upper_term += nt(local_up, upper)
            cross_term += nt(upper, local_low)
            lower_term += nt(local_low, lower)
        terms_ref[0, node] = upper_term
        terms_ref[1, node] = cross_term
        terms_ref[2, node] = lower_term


def body(
    n_row,
    n_col,
    ainv_top,
    block_owner,
    upper_list,
    upper_len,
    upper_panel,
    upper_dinv,
    lower_len,
    lower_panel,
    lower_parent,
    lower_dinv,
):
    width = upper_dinv.shape[-1]
    per_col = upper_dinv.shape[0]
    local_rows, local_cols = ainv_top.shape
    row_blocks = local_rows // width
    col_blocks = local_cols // width
    row_live = row_blocks // 2
    col_live = col_blocks // 2
    total = block_owner.shape[0]
    listed = upper_list.shape[1]
    mine = listed // n_row
    combos = 2 * per_col
    parts = n_row // combos
    piece = width // parts
    params = pltpu.CompilerParams(vmem_limit_bytes=40 * 1024 * 1024)
    here = lax.axis_index("row")

    every = jnp.arange(total, dtype=jnp.int32)
    places = jnp.arange(listed, dtype=jnp.int32)
    slots = jnp.sum(
        jnp.where(upper_list[:, :, None] == every, block_owner[None, None, :], 0), axis=2
    )
    rank = jnp.sum((slots[:, None, :] < slots[:, :, None]).astype(jnp.int32), axis=2)
    hit = rank[:, :, None] == places[None, None, :]
    order = jnp.sum(jnp.where(hit, places[None, :, None], 0), axis=1)
    sorted_slots = jnp.sum(jnp.where(hit, slots[:, :, None], 0), axis=1)
    live_up = (order < upper_len[:, None]).astype(jnp.int32)
    live_low = (order < lower_len[:, None]).astype(jnp.int32)
    all_slots = lax.all_gather(sorted_slots, "col", axis=0, tiled=True)

    panels = jnp.concatenate([upper_panel, lower_panel], axis=0)
    panels = panels.reshape(combos, mine, width, parts, piece)
    panels = panels.transpose(0, 3, 1, 2, 4).reshape(n_row, mine, width, piece)
    whole = lax.all_to_all(panels, "row", split_axis=0, concat_axis=0, tiled=True)
    whole = whole.reshape(listed, width, piece)
    combo = here // parts
    node = combo % per_col
    live_all = jnp.concatenate([live_up, live_low], axis=0)
    spread = pl.pallas_call(
        pick_kernel,
        out_shape=jax.ShapeDtypeStruct((listed, piece, width), jnp.float32),
        in_specs=[pl.BlockSpec(memory_space=SMEM)] * 2 + [pl.BlockSpec(memory_space=VMEM)],
        out_specs=pl.BlockSpec(memory_space=VMEM),
        compiler_params=params,
        name="pick",
    )(order[node], live_all[combo], whole)

    landed = lax.all_to_all(
        spread.reshape(n_col, col_live, piece, width), "col", split_axis=0, concat_axis=0, tiled=True
    )
    gathered = lax.all_gather(landed, "row", axis=0, tiled=False)
    row_at = lax.dynamic_slice_in_dim(all_slots, here * row_live, row_live, 1) - here * row_blocks
    col_here = lax.axis_index("col")
    col_at = lax.dynamic_slice_in_dim(all_slots, col_here * col_live, col_live, 1) - col_here * col_blocks
    live_width = row_live * width
    partial = pl.pallas_call(
        functools.partial(product_kernel, per_col),
        grid=(n_col,),
        out_shape=jax.ShapeDtypeStruct((n_col, combos, width, live_width), jnp.float32),
        in_specs=[
            pl.BlockSpec(memory_space=SMEM),
            pl.BlockSpec(memory_space=SMEM),
            pl.BlockSpec((local_rows, local_cols), lambda c: (0, 0)),
            pl.BlockSpec((n_row, 1, col_live, piece, width), lambda c: (0, c, 0, 0, 0)),
        ],
        out_specs=pl.BlockSpec((1, combos, width, live_width), lambda c: (c, 0, 0, 0)),
        scratch_shapes=[
            VMEM((col_blocks, row_blocks, width, width), jnp.bfloat16),
            VMEM((col_blocks, row_blocks, width, width), jnp.bfloat16),
        ],
        compiler_params=params,
        name="products",
    )(row_at, col_at, ainv_top, gathered)
    local = lax.all_to_all(
        spread.reshape(n_row, row_live, piece, width), "row", split_axis=0, concat_axis=0, tiled=True
    )
    sums = lax.psum_scatter(partial, "col", scatter_dimension=0, tiled=True)[0]

    mine_at = lax.dynamic_slice_in_dim(sorted_slots, here * row_live, row_live, 1) - here * row_blocks
    mine_up = lax.dynamic_slice_in_dim(live_up, here * row_live, row_live, 1)
    mine_low = lax.dynamic_slice_in_dim(live_low, here * row_live, row_live, 1)
    upper_rows, lower_rows, terms = pl.pallas_call(
        functools.partial(finish_kernel, per_col),
        out_shape=(
            jax.ShapeDtypeStruct((per_col, width, local_rows), jnp.float32),
            jax.ShapeDtypeStruct((per_col, width, local_rows), jnp.float32),
            jax.ShapeDtypeStruct((3, per_col, width, width), jnp.float32),
        ),
        in_specs=[pl.BlockSpec(memory_space=SMEM)] * 3 + [pl.BlockSpec(memory_space=VMEM)] * 3,
        out_specs=(pl.BlockSpec(memory_space=VMEM),) * 3,
        compiler_params=params,
        name="finish",
    )(mine_at, mine_up, mine_low, sums, local, lower_parent)
    totals = lax.psum(terms, "row")
    diag_up = upper_dinv - totals[0]
    parent_row = -(jnp.einsum("bij,bjk->bik", diag_up, lower_parent, precision=highest) + totals[1])
    diag_low = (
        lower_dinv
        - jnp.einsum("bji,bjk->bik", lower_parent, parent_row, precision=highest)
        - totals[2]
    )
    return (upper_rows, diag_up, lower_rows, parent_row, diag_low)


def solution(mesh):
    in_specs = (
        P("row", "col"),
        P(),
        P("col", None),
        P("col"),
        P("col", "row", None),
        P("col", None, None),
        P("col"),
        P("col", "row", None),
        P("col", None, None),
        P("col", None, None),
    )
    out_specs = (
        P("col", None, "row"),
        P("col", None, None),
        P("col", None, "row"),
        P("col", None, None),
        P("col", None, None),
    )
    inner = functools.partial(body, mesh.shape["row"], mesh.shape["col"])
    return jax.shard_map(inner, mesh=mesh, in_specs=in_specs, out_specs=out_specs, check_vma=False)
```

```python
import functools

import jax
import jax.numpy as jnp
from jax import lax
from jax.experimental import pallas as pl
from jax.experimental.pallas import tpu as pltpu
from jax.sharding import PartitionSpec as P

highest = lax.Precision.HIGHEST
VMEM = pltpu.VMEM
SMEM = pltpu.SMEM


def nt(left, right):
    return lax.dot_general(
        left, right, (((1,), (1,)), ((), ())), precision=highest, preferred_element_type=jnp.float32
    )


def nn(left, right):
    return lax.dot_general(
        left, right, (((1,), (0,)), ((), ())), precision=highest, preferred_element_type=jnp.float32
    )


def tn(left, right):
    return lax.dot_general(
        left, right, (((0,), (0,)), ((), ())), precision=highest, preferred_element_type=jnp.float32
    )


def split_bf16(value):
    high = value.astype(jnp.bfloat16)
    low = (value - high.astype(jnp.float32)).astype(jnp.bfloat16)
    return high, low


def mega_kernel(
    per_col, n_row, n_col,
    order_ref, live_ref, row_ref, col_ref, at_ref, up_ref, low_ref,
    panels_ref, ainv_ref, parent_ref, updinv_ref, lowdinv_ref,
    up_off_ref, up_diag_ref, low_off_ref, prow_ref, low_diag_ref,
    whole, spread, gathered, high_ref, low_part_ref, own, away, mate, line, local, terms, landed, totals,
    a_send, a_recv, c_send, c_recv, g_send, g_recv, l_send, l_recv,
    s_send, s_recv, z_send, z_recv, t_send, t_recv,
):
    me_r = lax.axis_index("row")
    me_c = lax.axis_index("col")
    chips = n_col // 2
    z = me_c // 2
    core = me_c % 2
    sibling = me_c + 1 - 2 * core
    combos = 2 * per_col
    parts = n_row // combos
    mine = panels_ref.shape[1]
    col_blocks, row_blocks, width, _ = high_ref.shape
    col_live = gathered.shape[2]
    row_live = local.shape[1]

    def remote(src, dst, send, recv, target):
        return pltpu.make_async_remote_copy(
            src_ref=src, dst_ref=dst, send_sem=send, recv_sem=recv,
            device_id=target, device_id_type=pl.DeviceIdType.MESH,
        )

    barrier = pltpu.get_barrier_semaphore()
    for d in range(1, n_row):
        pl.semaphore_signal(barrier, inc=1, device_id={"row": (me_r + d) % n_row},
                            device_id_type=pl.DeviceIdType.MESH)
    for d in range(1, n_col):
        pl.semaphore_signal(barrier, inc=1, device_id={"col": (me_c + d) % n_col},
                            device_id_type=pl.DeviceIdType.MESH)
    pl.semaphore_wait(barrier, n_row + n_col - 2)

    def share(peer, source):
        return remote(panels_ref.at[peer], whole.at[pl.ds(source * mine, mine)],
                      a_send.at[peer], a_recv.at[source], {"row": peer})

    for d in range(1, n_row):
        share((me_r + d) % n_row, me_r).start()
    whole[pl.ds(me_r * mine, mine)] = panels_ref[me_r]
    for cb in range(col_blocks):
        for rb in range(row_blocks):
            block = ainv_ref[rb * width:(rb + 1) * width, cb * width:(cb + 1) * width]
            high, low = split_bf16(block)
            high_ref[cb, rb] = high
            low_part_ref[cb, rb] = low
    for d in range(1, n_row):
        share(me_r, (me_r + d) % n_row).wait_recv()

    def pick(c):
        for s in range(col_live):
            place = c * col_live + s
            block = whole[order_ref[place]]
            spread[place] = jnp.where(live_ref[place] > 0, block, 0.0).T

    def ship(c, source):
        return remote(spread.at[pl.ds(c * col_live, col_live)], gathered.at[me_r, source],
                      c_send.at[c], c_recv.at[source], {"col": c})

    def pick_and_ship(c):
        pick(c)
        ship(c, me_c).start()

    def side_chip(t, side):
        chip = (1 - side) * (chips - 1 - t) + side * t
        active = jnp.where(side == 0, chip > z, chip < z)
        return chip, active

    pick(me_c)
    gathered[me_r, me_c] = spread[pl.ds(me_c * col_live, col_live)]

    def ship_step(i, carry):
        chip, active = side_chip(i // 2, i % 2)

        @pl.when(active)
        def _():
            pick_and_ship(2 * chip + core)
            pick_and_ship(2 * chip + 1 - core)

        return carry

    lax.fori_loop(0, 2 * chips, ship_step, 0)
    pick_and_ship(sibling)

    def pass_on(c, peer, source):
        return remote(gathered.at[source, c], gathered.at[source, c],
                      g_send.at[peer, c], g_recv.at[source, c], {"row": peer})

    def forward(c):
        for d in range(1, n_row):
            pass_on(c, (me_r + d) % n_row, me_r).start()

    forward(me_c)

    def forward_step(i, carry):
        chip, active = side_chip(i // 2, i % 2)

        @pl.when(active)
        def _():
            for c in (2 * chip + core, 2 * chip + 1 - core):
                ship(me_c, c).wait_recv()
                forward(c)

        return carry

    lax.fori_loop(0, 2 * chips, forward_step, 0)
    ship(me_c, sibling).wait_recv()
    forward(sibling)

    def local_copy(peer, source):
        return remote(spread.at[pl.ds(peer * row_live, row_live)], local.at[source],
                      l_send.at[peer], l_recv.at[source], {"row": peer})

    for d in range(1, n_row):
        local_copy((me_r + d) % n_row, me_r).start()
    local[me_r] = spread[pl.ds(me_r * row_live, row_live)]

    def product(c, chip, out):
        for d in range(1, n_row):
            pass_on(c, me_r, (me_r + d) % n_row).wait_recv()
        for node in range(per_col):
            rows = []
            for panel in range(2):
                for part in range(parts):
                    source = (panel * per_col + node) * parts + part
                    rows.append(jnp.concatenate([gathered[source, c, s] for s in range(col_live)], axis=1))
            left_high, left_low = split_bf16(jnp.concatenate(rows, axis=0))
            left_all = jnp.concatenate([left_high, left_high, left_low], axis=1)
            at = c * per_col + node
            cols = [col_ref[at, s] for s in range(col_live)]
            for rb in range(row_live):
                row = row_ref[at, rb]
                high = [high_ref[cb, row] for cb in cols]
                low = [low_part_ref[cb, row] for cb in cols]
                right = jnp.concatenate(high + low + high, axis=1)
                total = lax.dot_general(
                    left_all, right, (((1,), (1,)), ((), ())), preferred_element_type=jnp.float32
                )
                for panel in range(2):
                    out[chip, panel * per_col + node, :, rb * width:(rb + 1) * width] = (
                        -total[panel * width:(panel + 1) * width]
                    )

    def to_mate(chip):
        return remote(away.at[chip], mate.at[chip], s_send.at[chip], s_recv.at[chip], {"col": sibling})

    def both_products(chip):
        product(2 * chip + 1 - core, chip, away)
        to_mate(chip).start()
        product(2 * chip + core, chip, own)

    def onward(chip, s, side):
        slot = jnp.where((side == 1) & (z - 1 == chip), chips, chip)
        return remote(own.at[chip, s], line.at[slot, s], z_send.at[chip, s], z_recv.at[slot, s],
                      {"col": me_c + 2 - 4 * side})

    def arrived(slot, s):
        remote(own.at[0, s], line.at[slot, s], z_send.at[0, s], z_recv.at[slot, s],
               {"col": sibling}).wait_recv()

    def chunk_step(t, carry):
        def compute_side(side, inner):
            chip, active = side_chip(t, side)

            @pl.when(active)
            def _():
                both_products(chip)
                to_mate(chip).wait_recv()

            return inner

        def send_side(i, inner):
            s = i // 2
            side = i % 2
            chip, active = side_chip(t, side)

            @pl.when(active)
            def _():
                own[chip, s] = own[chip, s] + mate[chip, s]

                @pl.when(jnp.where(side == 0, z > 0, z < chips - 1))
                def _():
                    arrived(chip, s)
                    own[chip, s] = own[chip, s] + line[chip, s]

                onward(chip, s, side).start()

            return inner

        lax.fori_loop(0, 2, compute_side, 0)
        lax.fori_loop(0, 2 * combos, send_side, 0)
        return carry

    lax.fori_loop(0, chips, chunk_step, 0)
    both_products(z)
    to_mate(z).wait_recv()

    def last_step(s, carry):
        own[z, s] = own[z, s] + mate[z, s]

        @pl.when(z > 0)
        def _():
            arrived(z, s)
            own[z, s] = own[z, s] + line[z, s]

        @pl.when(z < chips - 1)
        def _():
            arrived(chips, s)
            own[z, s] = own[z, s] + line[chips, s]

        return carry

    lax.fori_loop(0, combos, last_step, 0)
    for d in range(1, n_row):
        local_copy(me_r, (me_r + d) % n_row).wait_recv()

    up_off_ref[...] = jnp.zeros_like(up_off_ref)
    low_off_ref[...] = jnp.zeros_like(low_off_ref)
    part_rows = width // n_row

    def full(combo, place):
        return jnp.concatenate([local[combo * parts + part, place] for part in range(parts)], axis=0)

    for node in range(per_col):
        sums = [jnp.zeros((width, width), jnp.float32)] * 3
        for place in range(row_live):
            span = slice(place * width, (place + 1) * width)
            upper = jnp.where(up_ref[node, place] > 0, own[z, node, :, span], 0.0)
            lower = own[z, per_col + node, :, span] - tn(parent_ref[node], upper)
            lower = jnp.where(low_ref[node, place] > 0, lower, 0.0)
            for block in range(row_blocks):
                here = at_ref[node, place] == block
                to = slice(block * width, (block + 1) * width)
                up_off_ref[node, :, to] = jnp.where(here, upper, up_off_ref[node, :, to])
                low_off_ref[node, :, to] = jnp.where(here, lower, low_off_ref[node, :, to])
            local_up = full(node, place)
            local_low = full(per_col + node, place)
            sums = [sums[0] + nt(local_up, upper), sums[1] + nt(upper, local_low),
                    sums[2] + nt(local_low, lower)]
        for kind in range(3):
            for j in range(n_row):
                terms[j, kind * per_col + node] = sums[kind][j * part_rows:(j + 1) * part_rows]

    def scatter(peer, source):
        return remote(terms.at[peer], landed.at[source], t_send.at[0, peer], t_recv.at[0, source],
                      {"row": peer})

    def spread_total(peer, source):
        return remote(totals.at[source], totals.at[source], t_send.at[1, peer], t_recv.at[1, source],
                      {"row": peer})

    for d in range(1, n_row):
        scatter((me_r + d) % n_row, me_r).start()
    landed[me_r] = terms[me_r]
    for d in range(1, n_row):
        scatter(me_r, (me_r + d) % n_row).wait_recv()
    total = landed[0]
    for j in range(1, n_row):
        total = total + landed[j]
    totals[me_r] = total
    for d in range(1, n_row):
        spread_total((me_r + d) % n_row, me_r).start()
    for d in range(1, n_row):
        spread_total(me_r, (me_r + d) % n_row).wait_recv()

    def summed(kind, node):
        return jnp.concatenate([totals[j, kind * per_col + node] for j in range(n_row)], axis=0)

    for node in range(per_col):
        parent = parent_ref[node]
        diag_up = updinv_ref[node] - summed(0, node)
        prow = -(nn(diag_up, parent) + summed(1, node))
        up_diag_ref[node] = diag_up
        prow_ref[node] = prow
        low_diag_ref[node] = lowdinv_ref[node] - tn(parent, prow) - summed(2, node)

    for d in range(1, n_row):
        peer = (me_r + d) % n_row
        share(peer, me_r).wait_send()
        local_copy(peer, me_r).wait_send()
        scatter(peer, me_r).wait_send()
        spread_total(peer, me_r).wait_send()
        for c in range(n_col):
            pass_on(c, peer, me_r).wait_send()
    for d in range(1, n_col):
        ship((me_c + d) % n_col, me_c).wait_send()
    for chip in range(chips):
        to_mate(chip).wait_send()

    def drain(i, carry):
        chip = i // combos

        @pl.when(chip != z)
        def _():
            onward(chip, i % combos, jnp.where(chip > z, 0, 1)).wait_send()

        return carry

    lax.fori_loop(0, chips * combos, drain, 0)


def body(
    n_row,
    n_col,
    ainv_top,
    block_owner,
    upper_list,
    upper_len,
    upper_panel,
    upper_dinv,
    lower_len,
    lower_panel,
    lower_parent,
    lower_dinv,
):
    width = upper_dinv.shape[-1]
    per_col = upper_dinv.shape[0]
    local_rows, local_cols = ainv_top.shape
    row_blocks = local_rows // width
    col_blocks = local_cols // width
    row_live = row_blocks // 2
    col_live = col_blocks // 2
    total = block_owner.shape[0]
    listed = upper_list.shape[1]
    mine = listed // n_row
    combos = 2 * per_col
    parts = n_row // combos
    piece = width // parts
    here = lax.axis_index("row")

    every = jnp.arange(total, dtype=jnp.int32)
    places = jnp.arange(listed, dtype=jnp.int32)
    slots = jnp.sum(
        jnp.where(upper_list[:, :, None] == every, block_owner[None, None, :], 0), axis=2
    )
    rank = jnp.sum((slots[:, None, :] < slots[:, :, None]).astype(jnp.int32), axis=2)
    hit = rank[:, :, None] == places[None, None, :]
    order = jnp.sum(jnp.where(hit, places[None, :, None], 0), axis=1)
    sorted_slots = jnp.sum(jnp.where(hit, slots[:, :, None], 0), axis=1)
    live_up = (order < upper_len[:, None]).astype(jnp.int32)
    live_low = (order < lower_len[:, None]).astype(jnp.int32)
    all_slots = lax.all_gather(sorted_slots, "col", axis=0, tiled=True)

    panels = jnp.concatenate([upper_panel, lower_panel], axis=0)
    panels = panels.reshape(combos, mine, width, parts, piece)
    panels = panels.transpose(0, 3, 1, 2, 4).reshape(n_row, mine, width, piece)
    combo = here // parts
    node = combo % per_col
    live_all = jnp.concatenate([live_up, live_low], axis=0)
    col_here = lax.axis_index("col")
    row_at = lax.dynamic_slice_in_dim(all_slots, here * row_live, row_live, 1) - here * row_blocks
    col_at = lax.dynamic_slice_in_dim(all_slots, col_here * col_live, col_live, 1) - col_here * col_blocks
    mine_at = lax.dynamic_slice_in_dim(sorted_slots, here * row_live, row_live, 1) - here * row_blocks
    mine_up = lax.dynamic_slice_in_dim(live_up, here * row_live, row_live, 1)
    mine_low = lax.dynamic_slice_in_dim(live_low, here * row_live, row_live, 1)
    chips = n_col // 2
    live_width = row_live * width
    f32 = jnp.float32
    dma = pltpu.SemaphoreType.DMA
    square = jax.ShapeDtypeStruct((per_col, width, width), f32)
    wide = jax.ShapeDtypeStruct((per_col, width, local_rows), f32)
    chunks = VMEM((chips, combos, width, live_width), f32)
    shares = VMEM((n_row, 3 * per_col, width // n_row, width), f32)
    return pl.pallas_call(
        functools.partial(mega_kernel, per_col, n_row, n_col),
        out_shape=(wide, square, wide, square, square),
        in_specs=[pl.BlockSpec(memory_space=SMEM)] * 7 + [pl.BlockSpec(memory_space=VMEM)] * 5,
        out_specs=(pl.BlockSpec(memory_space=VMEM),) * 5,
        scratch_shapes=[
            VMEM((listed, width, piece), f32),
            VMEM((listed, piece, width), f32),
            VMEM((n_row, n_col, col_live, piece, width), f32),
            VMEM((col_blocks, row_blocks, width, width), jnp.bfloat16),
            VMEM((col_blocks, row_blocks, width, width), jnp.bfloat16),
            chunks,
            chunks,
            chunks,
            VMEM((chips + 1, combos, width, live_width), f32),
            VMEM((n_row, row_live, piece, width), f32),
            shares,
            shares,
            shares,
            dma((n_row,)),
            dma((n_row,)),
            dma((n_col,)),
            dma((n_col,)),
            dma((n_row, n_col)),
            dma((n_row, n_col)),
            dma((n_row,)),
            dma((n_row,)),
            dma((chips,)),
            dma((chips,)),
            dma((chips, combos)),
            dma((chips + 1, combos)),
            dma((2, n_row)),
            dma((2, n_row)),
        ],
        compiler_params=pltpu.CompilerParams(
            collective_id=0, has_side_effects=True, vmem_limit_bytes=60 * 1024 * 1024
        ),
        name="selected_inverse",
    )(
        order[node], live_all[combo], row_at, col_at, mine_at, mine_up, mine_low,
        panels, ainv_top, lower_parent, upper_dinv, lower_dinv,
    )


def solution(mesh):
    in_specs = (
        P("row", "col"),
        P(),
        P("col", None),
        P("col"),
        P("col", "row", None),
        P("col", None, None),
        P("col"),
        P("col", "row", None),
        P("col", None, None),
        P("col", None, None),
    )
    out_specs = (
        P("col", None, "row"),
        P("col", None, None),
        P("col", None, "row"),
        P("col", None, None),
        P("col", None, None),
    )
    inner = functools.partial(body, mesh.shape["row"], mesh.shape["col"])
    return jax.shard_map(inner, mesh=mesh, in_specs=in_specs, out_specs=out_specs, check_vma=False)
```

```python
import functools

import jax
import jax.numpy as jnp
from jax import lax
from jax.experimental import pallas as pl
from jax.experimental.pallas import tpu as pltpu
from jax.sharding import PartitionSpec as P

highest = lax.Precision.HIGHEST
VMEM = pltpu.VMEM
SMEM = pltpu.SMEM


def nt(left, right):
    return lax.dot_general(
        left, right, (((1,), (1,)), ((), ())), precision=highest, preferred_element_type=jnp.float32
    )


def nn(left, right):
    return lax.dot_general(
        left, right, (((1,), (0,)), ((), ())), precision=highest, preferred_element_type=jnp.float32
    )


def tn(left, right):
    return lax.dot_general(
        left, right, (((0,), (0,)), ((), ())), precision=highest, preferred_element_type=jnp.float32
    )


def split_bf16(value):
    high = value.astype(jnp.bfloat16)
    low = (value - high.astype(jnp.float32)).astype(jnp.bfloat16)
    return high, low


def mega_kernel(
    per_col, n_row, n_col, n_panels,
    order_ref, up_len_ref, low_len_ref, tile_ref, *refs,
):
    panel_refs, refs = refs[:n_panels], refs[n_panels:]
    (
        ainv_hbm, parent_ref, up_ref, low_ref, totals_ref,
        whole, spread, gathered, ainv_ref, high_ref, low_part_ref, own, away, mate, line, local,
        terms, landed, totals, tiles, slots,
        a_send, a_recv, c_send, c_recv, g_send, g_recv, l_send, l_recv,
        s_send, s_recv, z_send, z_recv, t_send, t_recv, q_send, q_recv, own_sem, ainv_sem, slot_sem,
    ) = refs
    me_r = lax.axis_index("row")
    me_c = lax.axis_index("col")
    chips = n_col // 2
    z = me_c // 2
    core = me_c % 2
    sibling = me_c + 1 - 2 * core
    combos = 2 * per_col
    parts = n_row // combos
    mine = panel_refs[0].shape[1]
    col_blocks, row_blocks, width, _ = high_ref.shape
    col_live = gathered.shape[2]
    row_live = local.shape[1]

    def remote(src, dst, send, recv, target):
        return pltpu.make_async_remote_copy(
            src_ref=src, dst_ref=dst, send_sem=send, recv_sem=recv,
            device_id=target, device_id_type=pl.DeviceIdType.MESH,
        )

    barrier = pltpu.get_barrier_semaphore()
    for d in range(1, n_row):
        pl.semaphore_signal(barrier, inc=1, device_id={"row": (me_r + d) % n_row},
                            device_id_type=pl.DeviceIdType.MESH)
    for d in range(1, n_col):
        pl.semaphore_signal(barrier, inc=1, device_id={"col": (me_c + d) % n_col},
                            device_id_type=pl.DeviceIdType.MESH)
    pl.semaphore_wait(barrier, n_row + n_col - 2)

    def held(peer):
        if n_panels == 1:
            return panel_refs[0].at[peer]
        return panel_refs[peer // per_col].at[peer % per_col]

    def share(peer, source):
        return remote(held(peer), whole.at[pl.ds(source * mine, mine)],
                      a_send.at[peer], a_recv.at[source], {"row": peer})

    def keep(peer):
        return pltpu.make_async_copy(held(peer), whole.at[pl.ds(me_r * mine, mine)], own_sem)

    def each_peer(act):
        for peer in range(n_row):
            @pl.when(peer != me_r)
            def _():
                act(share(peer, me_r))

    def slot_copy(c, source):
        return remote(tile_ref, tiles.at[source], q_send.at[c], q_recv.at[source], {"col": c})

    each_peer(lambda copy: copy.start())
    for peer in range(n_row):
        @pl.when(peer == me_r)
        def _():
            keep(peer).start()
    fetch = pltpu.make_async_copy(ainv_hbm, ainv_ref, ainv_sem)
    fetch.start()
    for d in range(1, n_col):
        slot_copy((me_c + d) % n_col, me_c).start()
    tiles[me_c] = tile_ref[...]
    fetch.wait()
    for cb in range(col_blocks):
        for rb in range(row_blocks):
            block = ainv_ref[rb * width:(rb + 1) * width, cb * width:(cb + 1) * width]
            high, low = split_bf16(block)
            high_ref[cb, rb] = high
            low_part_ref[cb, rb] = low
    keep(0).wait()
    for d in range(1, n_row):
        share(0, (me_r + d) % n_row).wait_recv()

    my_combo = me_r // parts
    my_node = my_combo % per_col
    my_len = jnp.where(my_combo < per_col, up_len_ref[my_node], low_len_ref[my_node])

    def pick(c):
        for s in range(col_live):
            place = c * col_live + s
            listed_at = order_ref[my_node, place]
            spread[place] = jnp.where(listed_at < my_len, whole[listed_at], 0.0).T

    def ship(c, source):
        return remote(spread.at[pl.ds(c * col_live, col_live)], gathered.at[me_r, source],
                      c_send.at[c], c_recv.at[source], {"col": c})

    def pick_and_ship(c):
        pick(c)
        ship(c, me_c).start()

    def side_chip(t, side):
        chip = (1 - side) * (chips - 1 - t) + side * t
        active = jnp.where(side == 0, chip > z, chip < z)
        return chip, active

    pick(me_c)
    gathered[me_r, me_c] = spread[pl.ds(me_c * col_live, col_live)]

    def ship_step(i, carry):
        chip, active = side_chip(i // 2, i % 2)

        @pl.when(active)
        def _():
            pick_and_ship(2 * chip + core)
            pick_and_ship(2 * chip + 1 - core)

        return carry

    lax.fori_loop(0, 2 * chips, ship_step, 0)
    pick_and_ship(sibling)

    def pass_on(c, peer, source):
        return remote(gathered.at[source, c], gathered.at[source, c],
                      g_send.at[peer, c], g_recv.at[source, c], {"row": peer})

    def forward(c):
        for d in range(1, n_row):
            pass_on(c, (me_r + d) % n_row, me_r).start()

    forward(me_c)
    ship(me_c, sibling).wait_recv()
    forward(sibling)

    def forward_side(i, carry):
        chip, active = side_chip(i // 2, i % 2)

        @pl.when(active)
        def _():
            for c in (2 * chip + core, 2 * chip + 1 - core):
                ship(me_c, c).wait_recv()
                forward(c)

        return carry

    lax.fori_loop(0, 4, forward_side, 0)

    def local_copy(peer, source):
        return remote(spread.at[pl.ds(peer * row_live, row_live)], local.at[source],
                      l_send.at[peer], l_recv.at[source], {"row": peer})

    for d in range(1, n_row):
        local_copy((me_r + d) % n_row, me_r).start()
    local[me_r] = spread[pl.ds(me_r * row_live, row_live)]

    for d in range(1, n_col):
        slot_copy(me_c, (me_c + d) % n_col).wait_recv()
    to_scalars = pltpu.make_async_copy(tiles, slots, slot_sem)
    to_scalars.start()
    to_scalars.wait()

    def product(c, chip, out):
        for d in range(1, n_row):
            pass_on(c, me_r, (me_r + d) % n_row).wait_recv()
        for node in range(per_col):
            rows = []
            for panel in range(2):
                for part in range(parts):
                    source = (panel * per_col + node) * parts + part
                    rows.append(jnp.concatenate([gathered[source, c, s] for s in range(col_live)], axis=1))
            left_high, left_low = split_bf16(jnp.concatenate(rows, axis=0))
            left_all = jnp.concatenate([left_high, left_high, left_low], axis=1)
            cols = [lax.rem(slots[c, node, me_c * col_live + s], col_blocks) for s in range(col_live)]
            for rb in range(row_live):
                row = lax.rem(slots[c, node, me_r * row_live + rb], row_blocks)
                high = [high_ref[cb, row] for cb in cols]
                low = [low_part_ref[cb, row] for cb in cols]
                right = jnp.concatenate(high + low + high, axis=1)
                total = lax.dot_general(
                    left_all, right, (((1,), (1,)), ((), ())), preferred_element_type=jnp.float32
                )
                for panel in range(2):
                    out[chip, panel * per_col + node, :, rb * width:(rb + 1) * width] = (
                        -total[panel * width:(panel + 1) * width]
                    )

    def to_mate(chip):
        return remote(away.at[chip], mate.at[chip], s_send.at[chip], s_recv.at[chip], {"col": sibling})

    def both_products(chip):
        product(2 * chip + 1 - core, chip, away)
        to_mate(chip).start()
        product(2 * chip + core, chip, own)

    def onward(chip, s, side):
        slot = jnp.where((side == 1) & (z - 1 == chip), chips, chip)
        return remote(own.at[chip, s], line.at[slot, s], z_send.at[chip, s], z_recv.at[slot, s],
                      {"col": me_c + 2 - 4 * side})

    def arrived(slot, s):
        remote(own.at[0, s], line.at[slot, s], z_send.at[0, s], z_recv.at[slot, s],
               {"col": sibling}).wait_recv()

    def chunk_step(t, carry):
        def compute_side(side, inner):
            chip, active = side_chip(t, side)

            @pl.when(active)
            def _():
                both_products(chip)
                to_mate(chip).wait_recv()

            return inner

        def send_side(i, inner):
            s = i // 2
            side = i % 2
            chip, active = side_chip(t, side)

            @pl.when(active)
            def _():
                own[chip, s] = own[chip, s] + mate[chip, s]

                @pl.when(jnp.where(side == 0, z > 0, z < chips - 1))
                def _():
                    arrived(chip, s)
                    own[chip, s] = own[chip, s] + line[chip, s]

                onward(chip, s, side).start()

            return inner

        lax.fori_loop(0, 2, compute_side, 0)
        lax.fori_loop(0, 2 * combos, send_side, 0)
        lax.fori_loop(2 * t + 4, 2 * t + 6, forward_side, 0)
        return carry

    lax.fori_loop(0, chips, chunk_step, 0)
    both_products(z)
    to_mate(z).wait_recv()

    def last_step(s, carry):
        own[z, s] = own[z, s] + mate[z, s]

        @pl.when(z > 0)
        def _():
            arrived(z, s)
            own[z, s] = own[z, s] + line[z, s]

        @pl.when(z < chips - 1)
        def _():
            arrived(chips, s)
            own[z, s] = own[z, s] + line[chips, s]

        return carry

    part_rows = width // n_row
    rounds = ((0, 2 * per_col), (2 * per_col, per_col))

    def full(combo, place):
        return jnp.concatenate([local[combo * parts + part, place] for part in range(parts)], axis=0)

    def spans():
        return [(place, slice(place * width, (place + 1) * width)) for place in range(row_live)]

    def live(node, place, length_ref):
        return order_ref[node, me_r * row_live + place] < length_ref[node]

    def put(kind, node, value):
        for j in range(n_row):
            terms[j, kind * per_col + node] = value[j * part_rows:(j + 1) * part_rows]

    def scatter(at, peer, source):
        part = pl.ds(*rounds[at])
        return remote(terms.at[peer, part], landed.at[source, part], t_send.at[at, peer],
                      t_recv.at[at, source], {"row": peer})

    def spread_total(at, peer, source):
        part = pl.ds(*rounds[at])
        return remote(totals.at[source, part], totals.at[source, part], t_send.at[2 + at, peer],
                      t_recv.at[2 + at, source], {"row": peer})

    def start_round(at):
        for d in range(1, n_row):
            scatter(at, (me_r + d) % n_row, me_r).start()
        part = pl.ds(*rounds[at])
        landed[me_r, part] = terms[me_r, part]

    def sum_round(at):
        for d in range(1, n_row):
            scatter(at, me_r, (me_r + d) % n_row).wait_recv()
        part = pl.ds(*rounds[at])
        total = landed[0, part]
        for j in range(1, n_row):
            total = total + landed[j, part]
        totals[me_r, part] = total
        for d in range(1, n_row):
            spread_total(at, (me_r + d) % n_row, me_r).start()

    for d in range(1, n_row):
        local_copy(me_r, (me_r + d) % n_row).wait_recv()
    lax.fori_loop(0, per_col, last_step, 0)
    for node in range(per_col):
        upper_term = jnp.zeros((width, width), jnp.float32)
        cross_term = jnp.zeros((width, width), jnp.float32)
        for place, span in spans():
            upper = jnp.where(live(node, place, up_len_ref), own[z, node, :, span], 0.0)
            up_ref[node, :, span] = upper
            upper_term = upper_term + nt(full(node, place), upper)
            cross_term = cross_term + nt(upper, full(per_col + node, place))
        put(0, node, upper_term)
        put(1, node, cross_term)
    start_round(0)
    for node in range(per_col):
        low_ref[node] = tn(parent_ref[node], up_ref[node])
    lax.fori_loop(per_col, combos, last_step, 0)
    for node in range(per_col):
        lower_term = jnp.zeros((width, width), jnp.float32)
        for place, span in spans():
            lower = own[z, per_col + node, :, span] - low_ref[node, :, span]
            lower = jnp.where(live(node, place, low_len_ref), lower, 0.0)
            low_ref[node, :, span] = lower
            lower_term = lower_term + nt(full(per_col + node, place), lower)
        put(2, node, lower_term)
    start_round(1)
    sum_round(0)
    sum_round(1)
    for at in range(2):
        for d in range(1, n_row):
            spread_total(at, me_r, (me_r + d) % n_row).wait_recv()
    totals_ref[...] = totals[...]

    for d in range(1, n_row):
        peer = (me_r + d) % n_row
        local_copy(peer, me_r).wait_send()
        for at in range(2):
            scatter(at, peer, me_r).wait_send()
            spread_total(at, peer, me_r).wait_send()
        for c in range(n_col):
            pass_on(c, peer, me_r).wait_send()
    for d in range(1, n_col):
        ship((me_c + d) % n_col, me_c).wait_send()
        slot_copy((me_c + d) % n_col, me_c).wait_send()
    each_peer(lambda copy: copy.wait_send())
    for chip in range(chips):
        to_mate(chip).wait_send()

    def drain(i, carry):
        chip = i // combos

        @pl.when(chip != z)
        def _():
            onward(chip, i % combos, jnp.where(chip > z, 0, 1)).wait_send()

        return carry

    lax.fori_loop(0, chips * combos, drain, 0)


def write_kernel(row_blocks, slot_ref, up_ref, low_ref, totals_ref, parent_ref, updinv_ref, lowdinv_ref,
                 up_off_ref, up_diag_ref, low_off_ref, prow_ref, low_diag_ref):
    per_col, width, _ = parent_ref.shape
    n_row = totals_ref.shape[0]
    row_live = up_ref.shape[2] // width
    up_off_ref[...] = jnp.zeros_like(up_off_ref)
    low_off_ref[...] = jnp.zeros_like(low_off_ref)

    def summed(kind, node):
        return jnp.concatenate([totals_ref[j, kind * per_col + node] for j in range(n_row)], axis=0)

    for node in range(per_col):
        for place in range(row_live):
            span = slice(place * width, (place + 1) * width)
            block = lax.rem(slot_ref[node, lax.axis_index("row") * row_live + place], row_blocks)
            at = pl.ds(pl.multiple_of(block * width, width), width)
            up_off_ref[node, :, at] = up_ref[node, :, span]
            low_off_ref[node, :, at] = low_ref[node, :, span]
        parent = parent_ref[node]
        diag_up = updinv_ref[node] - summed(0, node)
        prow = -(nn(diag_up, parent) + summed(1, node))
        up_diag_ref[node] = diag_up
        prow_ref[node] = prow
        low_diag_ref[node] = lowdinv_ref[node] - tn(parent, prow) - summed(2, node)


def body(
    n_row,
    n_col,
    ainv_top,
    block_owner,
    upper_list,
    upper_len,
    upper_panel,
    upper_dinv,
    lower_len,
    lower_panel,
    lower_parent,
    lower_dinv,
):
    width = upper_dinv.shape[-1]
    per_col = upper_dinv.shape[0]
    local_rows, local_cols = ainv_top.shape
    row_blocks = local_rows // width
    col_blocks = local_cols // width
    row_live = row_blocks // 2
    col_live = col_blocks // 2
    total = block_owner.shape[0]
    listed = upper_list.shape[1]
    mine = listed // n_row
    combos = 2 * per_col
    parts = n_row // combos
    piece = width // parts

    every = jnp.arange(total, dtype=jnp.int32)
    places = jnp.arange(listed, dtype=jnp.int32)
    slots = jnp.sum(
        jnp.where(upper_list[:, :, None] == every, block_owner[None, None, :], 0), axis=2
    )
    rank = jnp.sum((slots[:, None, :] < slots[:, :, None]).astype(jnp.int32), axis=2)
    hit = rank[:, :, None] == places[None, None, :]
    order = jnp.sum(jnp.where(hit, places[None, :, None], 0), axis=1)
    sorted_slots = jnp.sum(jnp.where(hit, slots[:, :, None], 0), axis=1)
    tile = jnp.pad(sorted_slots, ((0, 8 - per_col), (0, 128 - listed)))

    if parts == 1:
        panels = tuple(panel.reshape(per_col, mine, width, width) for panel in (upper_panel, lower_panel))
    else:
        both = jnp.concatenate([upper_panel, lower_panel], axis=0)
        both = both.reshape(combos, mine, width, parts, piece)
        panels = (both.transpose(0, 3, 1, 2, 4).reshape(n_row, mine, width, piece),)
    chips = n_col // 2
    live_width = row_live * width
    f32 = jnp.float32
    dma = pltpu.SemaphoreType.DMA
    square = jax.ShapeDtypeStruct((per_col, width, width), f32)
    wide = jax.ShapeDtypeStruct((per_col, width, local_rows), f32)
    chunks = VMEM((chips, combos, width, live_width), f32)
    shares = VMEM((n_row, 3 * per_col, width // n_row, width), f32)
    rows = jax.ShapeDtypeStruct((per_col, width, live_width), f32)
    upper_rows, lower_rows, totals = pl.pallas_call(
        functools.partial(mega_kernel, per_col, n_row, n_col, len(panels)),
        out_shape=(rows, rows, jax.ShapeDtypeStruct((n_row, 3 * per_col, width // n_row, width), f32)),
        in_specs=(
            [pl.BlockSpec(memory_space=SMEM)] * 3
            + [pl.BlockSpec(memory_space=VMEM)]
            + [pl.BlockSpec(memory_space=pl.ANY)] * (len(panels) + 1)
            + [pl.BlockSpec(memory_space=VMEM)]
        ),
        out_specs=(pl.BlockSpec(memory_space=VMEM),) * 3,
        scratch_shapes=[
            VMEM((listed, width, piece), f32),
            VMEM((listed, piece, width), f32),
            VMEM((n_row, n_col, col_live, piece, width), f32),
            VMEM((local_rows, local_cols), f32),
            VMEM((col_blocks, row_blocks, width, width), jnp.bfloat16),
            VMEM((col_blocks, row_blocks, width, width), jnp.bfloat16),
            chunks,
            chunks,
            chunks,
            VMEM((chips + 1, combos, width, live_width), f32),
            VMEM((n_row, row_live, piece, width), f32),
            shares,
            shares,
            shares,
            VMEM((n_col, 8, 128), jnp.int32),
            SMEM((n_col, 8, 128), jnp.int32),
            dma((n_row,)),
            dma((n_row,)),
            dma((n_col,)),
            dma((n_col,)),
            dma((n_row, n_col)),
            dma((n_row, n_col)),
            dma((n_row,)),
            dma((n_row,)),
            dma((chips,)),
            dma((chips,)),
            dma((chips, combos)),
            dma((chips + 1, combos)),
            dma((4, n_row)),
            dma((4, n_row)),
            dma((n_col,)),
            dma((n_col,)),
            dma(()),
            dma(()),
            dma(()),
        ],
        compiler_params=pltpu.CompilerParams(
            collective_id=0, has_side_effects=True, vmem_limit_bytes=60 * 1024 * 1024
        ),
        name="selected_inverse",
    )(order, upper_len, lower_len, tile, *panels, ainv_top, lower_parent)
    return pl.pallas_call(
        functools.partial(write_kernel, row_blocks),
        out_shape=(wide, square, wide, square, square),
        in_specs=[pl.BlockSpec(memory_space=SMEM)] + [pl.BlockSpec(memory_space=VMEM)] * 6,
        out_specs=(pl.BlockSpec(memory_space=VMEM),) * 5,
        compiler_params=pltpu.CompilerParams(vmem_limit_bytes=32 * 1024 * 1024),
        name="write_out",
    )(sorted_slots, upper_rows, lower_rows, totals, lower_parent, upper_dinv, lower_dinv)


def solution(mesh):
    in_specs = (
        P("row", "col"),
        P(),
        P("col", None),
        P("col"),
        P("col", "row", None),
        P("col", None, None),
        P("col"),
        P("col", "row", None),
        P("col", None, None),
        P("col", None, None),
    )
    out_specs = (
        P("col", None, "row"),
        P("col", None, None),
        P("col", None, "row"),
        P("col", None, None),
        P("col", None, None),
    )
    inner = functools.partial(body, mesh.shape["row"], mesh.shape["col"])
    return jax.shard_map(inner, mesh=mesh, in_specs=in_specs, out_specs=out_specs, check_vma=False)
```

```python
import functools

import jax
import jax.numpy as jnp
from jax import lax
from jax.experimental import pallas as pl
from jax.experimental.pallas import tpu as pltpu
from jax.sharding import PartitionSpec as P

highest = lax.Precision.HIGHEST
VMEM = pltpu.VMEM
SMEM = pltpu.SMEM


def nt(left, right):
    return lax.dot_general(
        left, right, (((1,), (1,)), ((), ())), precision=highest, preferred_element_type=jnp.float32
    )


def nn(left, right):
    return lax.dot_general(
        left, right, (((1,), (0,)), ((), ())), precision=highest, preferred_element_type=jnp.float32
    )


def tn(left, right):
    return lax.dot_general(
        left, right, (((0,), (0,)), ((), ())), precision=highest, preferred_element_type=jnp.float32
    )


def split_bf16(value):
    high = value.astype(jnp.bfloat16)
    low = (value - high.astype(jnp.float32)).astype(jnp.bfloat16)
    return high, low


def mega_kernel(
    per_col, n_row, n_col, n_panels,
    order_ref, up_len_ref, low_len_ref, tile_ref, *refs,
):
    panel_refs, refs = refs[:n_panels], refs[n_panels:]
    (
        ainv_hbm, parent_ref, up_ref, low_ref, totals_ref,
        whole, spread, gathered, ainv_ref, high_ref, low_part_ref, own, away, mate, line, local,
        terms, landed, totals, tiles, slots,
        a_send, a_recv, c_send, c_recv, g_send, g_recv, l_send, l_recv,
        s_send, s_recv, z_send, z_recv, t_send, t_recv, q_send, q_recv, own_sem, ainv_sem, slot_sem,
    ) = refs
    me_r = lax.axis_index("row")
    me_c = lax.axis_index("col")
    chips = n_col // 2
    z = me_c // 2
    core = me_c % 2
    sibling = me_c + 1 - 2 * core
    combos = 2 * per_col
    parts = n_row // combos
    mine = panel_refs[0].shape[1]
    col_blocks, row_blocks, width, _ = high_ref.shape
    col_live = gathered.shape[2]
    row_live = local.shape[1]

    def remote(src, dst, send, recv, target):
        return pltpu.make_async_remote_copy(
            src_ref=src, dst_ref=dst, send_sem=send, recv_sem=recv,
            device_id=target, device_id_type=pl.DeviceIdType.MESH,
        )

    barrier = pltpu.get_barrier_semaphore()
    for d in range(1, n_row):
        pl.semaphore_signal(barrier, inc=1, device_id={"row": (me_r + d) % n_row},
                            device_id_type=pl.DeviceIdType.MESH)
    for d in range(1, n_col):
        pl.semaphore_signal(barrier, inc=1, device_id={"col": (me_c + d) % n_col},
                            device_id_type=pl.DeviceIdType.MESH)
    pl.semaphore_wait(barrier, n_row + n_col - 2)

    def held(peer):
        if n_panels == 1:
            return panel_refs[0].at[peer]
        return panel_refs[peer // per_col].at[peer % per_col]

    def share(peer, source):
        return remote(held(peer), whole.at[pl.ds(source * mine, mine)],
                      a_send.at[peer], a_recv.at[source], {"row": peer})

    def keep(peer):
        return pltpu.make_async_copy(held(peer), whole.at[pl.ds(me_r * mine, mine)], own_sem)

    def each_peer(act):
        for peer in range(n_row):
            @pl.when(peer != me_r)
            def _():
                act(share(peer, me_r))

    def slot_copy(c, source):
        return remote(tile_ref, tiles.at[source], q_send.at[c], q_recv.at[source], {"col": c})

    each_peer(lambda copy: copy.start())
    for peer in range(n_row):
        @pl.when(peer == me_r)
        def _():
            keep(peer).start()
    fetch = pltpu.make_async_copy(ainv_hbm, ainv_ref, ainv_sem)
    fetch.start()
    for d in range(1, n_col):
        slot_copy((me_c + d) % n_col, me_c).start()
    tiles[me_c] = tile_ref[...]
    fetch.wait()
    for cb in range(col_blocks):
        for rb in range(row_blocks):
            block = ainv_ref[rb * width:(rb + 1) * width, cb * width:(cb + 1) * width]
            high, low = split_bf16(block)
            high_ref[cb, rb] = high
            low_part_ref[cb, rb] = low
    keep(0).wait()
    for d in range(1, n_row):
        share(0, (me_r + d) % n_row).wait_recv()

    my_combo = me_r // parts
    my_node = my_combo % per_col
    my_len = jnp.where(my_combo < per_col, up_len_ref[my_node], low_len_ref[my_node])

    def pick(c):
        for s in range(col_live):
            place = c * col_live + s
            listed_at = order_ref[my_node, place]
            spread[place] = jnp.where(listed_at < my_len, whole[listed_at], 0.0).T

    def ship(c, source):
        return remote(spread.at[pl.ds(c * col_live, col_live)], gathered.at[me_r, source],
                      c_send.at[c], c_recv.at[source], {"col": c})

    def pick_and_ship(c):
        pick(c)
        ship(c, me_c).start()

    def side_chip(t, side):
        chip = (1 - side) * (chips - 1 - t) + side * t
        active = jnp.where(side == 0, chip > z, chip < z)
        return chip, active

    pick(me_c)
    gathered[me_r, me_c] = spread[pl.ds(me_c * col_live, col_live)]

    def ship_step(i, carry):
        chip, active = side_chip(i // 2, i % 2)

        @pl.when(active)
        def _():
            pick_and_ship(2 * chip + core)
            pick_and_ship(2 * chip + 1 - core)

        return carry

    lax.fori_loop(0, 2 * chips, ship_step, 0)
    pick_and_ship(sibling)

    def pass_on(c, peer, source):
        return remote(gathered.at[source, c], gathered.at[source, c],
                      g_send.at[peer, c], g_recv.at[source, c], {"row": peer})

    def forward(c):
        for d in range(1, n_row):
            pass_on(c, (me_r + d) % n_row, me_r).start()

    forward(me_c)
    ship(me_c, sibling).wait_recv()
    forward(sibling)

    def forward_side(i, carry):
        chip, active = side_chip(i // 2, i % 2)

        @pl.when(active)
        def _():
            for c in (2 * chip + core, 2 * chip + 1 - core):
                ship(me_c, c).wait_recv()
                forward(c)

        return carry

    lax.fori_loop(0, 4, forward_side, 0)

    def local_copy(peer, source):
        return remote(spread.at[pl.ds(peer * row_live, row_live)], local.at[source],
                      l_send.at[peer], l_recv.at[source], {"row": peer})

    for d in range(1, n_row):
        local_copy((me_r + d) % n_row, me_r).start()
    local[me_r] = spread[pl.ds(me_r * row_live, row_live)]

    for d in range(1, n_col):
        slot_copy(me_c, (me_c + d) % n_col).wait_recv()
    to_scalars = pltpu.make_async_copy(tiles, slots, slot_sem)
    to_scalars.start()
    to_scalars.wait()

    def product(c, chip, out, send=None):
        for d in range(1, n_row):
            pass_on(c, me_r, (me_r + d) % n_row).wait_recv()
        for node in range(per_col):
            rows = []
            for panel in range(2):
                for part in range(parts):
                    source = (panel * per_col + node) * parts + part
                    rows.append(jnp.concatenate([gathered[source, c, s] for s in range(col_live)], axis=1))
            left_high, left_low = split_bf16(jnp.concatenate(rows, axis=0))
            left_all = jnp.concatenate([left_high, left_high, left_low], axis=1)
            cols = [lax.rem(slots[c, node, me_c * col_live + s], col_blocks) for s in range(col_live)]
            for rb in range(row_live):
                row = lax.rem(slots[c, node, me_r * row_live + rb], row_blocks)
                high = [high_ref[cb, row] for cb in cols]
                low = [low_part_ref[cb, row] for cb in cols]
                right = jnp.concatenate(high + low + high, axis=1)
                total = lax.dot_general(
                    left_all, right, (((1,), (1,)), ((), ())), preferred_element_type=jnp.float32
                )
                for panel in range(2):
                    out[chip, panel * per_col + node, :, rb * width:(rb + 1) * width] = (
                        -total[panel * width:(panel + 1) * width]
                    )
            if send is not None:
                for panel in range(2):
                    send(chip, panel * per_col + node).start()

    def to_mate(chip, s):
        return remote(away.at[chip, s], mate.at[chip, s], s_send.at[chip, s], s_recv.at[chip, s],
                      {"col": sibling})

    def both_products(chip):
        product(2 * chip + 1 - core, chip, away, to_mate)
        product(2 * chip + core, chip, own)

    def onward(chip, s, side):
        slot = jnp.where((side == 1) & (z - 1 == chip), chips, chip)
        return remote(own.at[chip, s], line.at[slot, s], z_send.at[chip, s], z_recv.at[slot, s],
                      {"col": me_c + 2 - 4 * side})

    def arrived(slot, s):
        remote(own.at[0, s], line.at[slot, s], z_send.at[0, s], z_recv.at[slot, s],
               {"col": sibling}).wait_recv()

    def chunk_step(t, carry):
        def compute_side(side, inner):
            chip, active = side_chip(t, side)

            @pl.when(active)
            def _():
                both_products(chip)

            return inner

        def send_side(i, inner):
            s = i // 2
            side = i % 2
            chip, active = side_chip(t, side)

            @pl.when(active)
            def _():
                to_mate(chip, s).wait_recv()
                own[chip, s] = own[chip, s] + mate[chip, s]

                @pl.when(jnp.where(side == 0, z > 0, z < chips - 1))
                def _():
                    arrived(chip, s)
                    own[chip, s] = own[chip, s] + line[chip, s]

                onward(chip, s, side).start()

            return inner

        lax.fori_loop(0, 2, compute_side, 0)
        lax.fori_loop(0, 2 * combos, send_side, 0)
        lax.fori_loop(2 * t + 4, 2 * t + 6, forward_side, 0)
        return carry

    lax.fori_loop(0, chips, chunk_step, 0)
    both_products(z)

    def last_step(s, carry):
        to_mate(z, s).wait_recv()
        own[z, s] = own[z, s] + mate[z, s]

        @pl.when(z > 0)
        def _():
            arrived(z, s)
            own[z, s] = own[z, s] + line[z, s]

        @pl.when(z < chips - 1)
        def _():
            arrived(chips, s)
            own[z, s] = own[z, s] + line[chips, s]

        return carry

    part_rows = width // n_row
    rounds = ((0, 2 * per_col), (2 * per_col, per_col))

    def full(combo, place):
        return jnp.concatenate([local[combo * parts + part, place] for part in range(parts)], axis=0)

    def spans():
        return [(place, slice(place * width, (place + 1) * width)) for place in range(row_live)]

    def live(node, place, length_ref):
        return order_ref[node, me_r * row_live + place] < length_ref[node]

    def put(kind, node, value):
        for j in range(n_row):
            terms[j, kind * per_col + node] = value[j * part_rows:(j + 1) * part_rows]

    def scatter(at, peer, source):
        part = pl.ds(*rounds[at])
        return remote(terms.at[peer, part], landed.at[source, part], t_send.at[at, peer],
                      t_recv.at[at, source], {"row": peer})

    def spread_total(at, peer, source):
        part = pl.ds(*rounds[at])
        return remote(totals.at[source, part], totals.at[source, part], t_send.at[2 + at, peer],
                      t_recv.at[2 + at, source], {"row": peer})

    def start_round(at):
        for d in range(1, n_row):
            scatter(at, (me_r + d) % n_row, me_r).start()
        part = pl.ds(*rounds[at])
        landed[me_r, part] = terms[me_r, part]

    def sum_round(at):
        for d in range(1, n_row):
            scatter(at, me_r, (me_r + d) % n_row).wait_recv()
        part = pl.ds(*rounds[at])
        total = landed[0, part]
        for j in range(1, n_row):
            total = total + landed[j, part]
        totals[me_r, part] = total
        for d in range(1, n_row):
            spread_total(at, (me_r + d) % n_row, me_r).start()

    for d in range(1, n_row):
        local_copy(me_r, (me_r + d) % n_row).wait_recv()
    lax.fori_loop(0, per_col, last_step, 0)
    for node in range(per_col):
        upper_term = jnp.zeros((width, width), jnp.float32)
        cross_term = jnp.zeros((width, width), jnp.float32)
        for place, span in spans():
            upper = jnp.where(live(node, place, up_len_ref), own[z, node, :, span], 0.0)
            up_ref[node, :, span] = upper
            upper_term = upper_term + nt(full(node, place), upper)
            cross_term = cross_term + nt(upper, full(per_col + node, place))
        put(0, node, upper_term)
        put(1, node, cross_term)
    start_round(0)
    for node in range(per_col):
        low_ref[node] = tn(parent_ref[node], up_ref[node])
    for node in range(per_col):
        last_step(per_col + node, 0)
        lower_term = jnp.zeros((width, width), jnp.float32)
        for place, span in spans():
            lower = own[z, per_col + node, :, span] - low_ref[node, :, span]
            lower = jnp.where(live(node, place, low_len_ref), lower, 0.0)
            low_ref[node, :, span] = lower
            lower_term = lower_term + nt(full(per_col + node, place), lower)
        put(2, node, lower_term)
    start_round(1)
    sum_round(0)
    sum_round(1)
    for at in range(2):
        for d in range(1, n_row):
            spread_total(at, me_r, (me_r + d) % n_row).wait_recv()
    totals_ref[...] = totals[...]

    for d in range(1, n_row):
        peer = (me_r + d) % n_row
        local_copy(peer, me_r).wait_send()
        for at in range(2):
            scatter(at, peer, me_r).wait_send()
            spread_total(at, peer, me_r).wait_send()
        for c in range(n_col):
            pass_on(c, peer, me_r).wait_send()
    for d in range(1, n_col):
        ship((me_c + d) % n_col, me_c).wait_send()
        slot_copy((me_c + d) % n_col, me_c).wait_send()
    each_peer(lambda copy: copy.wait_send())

    def drain(i, carry):
        chip = i // combos
        to_mate(chip, i % combos).wait_send()

        @pl.when(chip != z)
        def _():
            onward(chip, i % combos, jnp.where(chip > z, 0, 1)).wait_send()

        return carry

    lax.fori_loop(0, chips * combos, drain, 0)


def write_kernel(row_blocks, slot_ref, up_ref, low_ref, totals_ref, parent_ref, updinv_ref, lowdinv_ref,
                 up_off_ref, up_diag_ref, low_off_ref, prow_ref, low_diag_ref):
    per_col, width, _ = parent_ref.shape
    n_row = totals_ref.shape[0]
    row_live = up_ref.shape[2] // width
    up_off_ref[...] = jnp.zeros_like(up_off_ref)
    low_off_ref[...] = jnp.zeros_like(low_off_ref)

    def summed(kind, node):
        return jnp.concatenate([totals_ref[j, kind * per_col + node] for j in range(n_row)], axis=0)

    for node in range(per_col):
        for place in range(row_live):
            span = slice(place * width, (place + 1) * width)
            block = lax.rem(slot_ref[node, lax.axis_index("row") * row_live + place], row_blocks)
            at = pl.ds(pl.multiple_of(block * width, width), width)
            up_off_ref[node, :, at] = up_ref[node, :, span]
            low_off_ref[node, :, at] = low_ref[node, :, span]
        parent = parent_ref[node]
        diag_up = updinv_ref[node] - summed(0, node)
        prow = -(nn(diag_up, parent) + summed(1, node))
        up_diag_ref[node] = diag_up
        prow_ref[node] = prow
        low_diag_ref[node] = lowdinv_ref[node] - tn(parent, prow) - summed(2, node)


def body(
    n_row,
    n_col,
    ainv_top,
    block_owner,
    upper_list,
    upper_len,
    upper_panel,
    upper_dinv,
    lower_len,
    lower_panel,
    lower_parent,
    lower_dinv,
):
    width = upper_dinv.shape[-1]
    per_col = upper_dinv.shape[0]
    local_rows, local_cols = ainv_top.shape
    row_blocks = local_rows // width
    col_blocks = local_cols // width
    row_live = row_blocks // 2
    col_live = col_blocks // 2
    total = block_owner.shape[0]
    listed = upper_list.shape[1]
    mine = listed // n_row
    combos = 2 * per_col
    parts = n_row // combos
    piece = width // parts

    every = jnp.arange(total, dtype=jnp.int32)
    places = jnp.arange(listed, dtype=jnp.int32)
    slots = jnp.sum(
        jnp.where(upper_list[:, :, None] == every, block_owner[None, None, :], 0), axis=2
    )
    rank = jnp.sum((slots[:, None, :] < slots[:, :, None]).astype(jnp.int32), axis=2)
    hit = rank[:, :, None] == places[None, None, :]
    order = jnp.sum(jnp.where(hit, places[None, :, None], 0), axis=1)
    sorted_slots = jnp.sum(jnp.where(hit, slots[:, :, None], 0), axis=1)
    tile = jnp.pad(sorted_slots, ((0, 8 - per_col), (0, 128 - listed)))

    if parts == 1:
        panels = tuple(panel.reshape(per_col, mine, width, width) for panel in (upper_panel, lower_panel))
    else:
        both = jnp.concatenate([upper_panel, lower_panel], axis=0)
        both = both.reshape(combos, mine, width, parts, piece)
        panels = (both.transpose(0, 3, 1, 2, 4).reshape(n_row, mine, width, piece),)
    chips = n_col // 2
    live_width = row_live * width
    f32 = jnp.float32
    dma = pltpu.SemaphoreType.DMA
    square = jax.ShapeDtypeStruct((per_col, width, width), f32)
    wide = jax.ShapeDtypeStruct((per_col, width, local_rows), f32)
    chunks = VMEM((chips, combos, width, live_width), f32)
    shares = VMEM((n_row, 3 * per_col, width // n_row, width), f32)
    rows = jax.ShapeDtypeStruct((per_col, width, live_width), f32)
    upper_rows, lower_rows, totals = pl.pallas_call(
        functools.partial(mega_kernel, per_col, n_row, n_col, len(panels)),
        out_shape=(rows, rows, jax.ShapeDtypeStruct((n_row, 3 * per_col, width // n_row, width), f32)),
        in_specs=(
            [pl.BlockSpec(memory_space=SMEM)] * 3
            + [pl.BlockSpec(memory_space=VMEM)]
            + [pl.BlockSpec(memory_space=pl.ANY)] * (len(panels) + 1)
            + [pl.BlockSpec(memory_space=VMEM)]
        ),
        out_specs=(pl.BlockSpec(memory_space=VMEM),) * 3,
        scratch_shapes=[
            VMEM((listed, width, piece), f32),
            VMEM((listed, piece, width), f32),
            VMEM((n_row, n_col, col_live, piece, width), f32),
            VMEM((local_rows, local_cols), f32),
            VMEM((col_blocks, row_blocks, width, width), jnp.bfloat16),
            VMEM((col_blocks, row_blocks, width, width), jnp.bfloat16),
            chunks,
            chunks,
            chunks,
            VMEM((chips + 1, combos, width, live_width), f32),
            VMEM((n_row, row_live, piece, width), f32),
            shares,
            shares,
            shares,
            VMEM((n_col, 8, 128), jnp.int32),
            SMEM((n_col, 8, 128), jnp.int32),
            dma((n_row,)),
            dma((n_row,)),
            dma((n_col,)),
            dma((n_col,)),
            dma((n_row, n_col)),
            dma((n_row, n_col)),
            dma((n_row,)),
            dma((n_row,)),
            dma((chips, combos)),
            dma((chips, combos)),
            dma((chips, combos)),
            dma((chips + 1, combos)),
            dma((4, n_row)),
            dma((4, n_row)),
            dma((n_col,)),
            dma((n_col,)),
            dma(()),
            dma(()),
            dma(()),
        ],
        compiler_params=pltpu.CompilerParams(
            collective_id=0, has_side_effects=True, vmem_limit_bytes=60 * 1024 * 1024
        ),
        name="selected_inverse",
    )(order, upper_len, lower_len, tile, *panels, ainv_top, lower_parent)
    return pl.pallas_call(
        functools.partial(write_kernel, row_blocks),
        out_shape=(wide, square, wide, square, square),
        in_specs=[pl.BlockSpec(memory_space=SMEM)] + [pl.BlockSpec(memory_space=VMEM)] * 6,
        out_specs=(pl.BlockSpec(memory_space=VMEM),) * 5,
        compiler_params=pltpu.CompilerParams(vmem_limit_bytes=60 * 1024 * 1024),
        name="write_out",
    )(sorted_slots, upper_rows, lower_rows, totals, lower_parent, upper_dinv, lower_dinv)


def solution(mesh):
    in_specs = (
        P("row", "col"),
        P(),
        P("col", None),
        P("col"),
        P("col", "row", None),
        P("col", None, None),
        P("col"),
        P("col", "row", None),
        P("col", None, None),
        P("col", None, None),
    )
    out_specs = (
        P("col", None, "row"),
        P("col", None, None),
        P("col", None, "row"),
        P("col", None, None),
        P("col", None, None),
    )
    inner = functools.partial(body, mesh.shape["row"], mesh.shape["col"])
    return jax.shard_map(inner, mesh=mesh, in_specs=in_specs, out_specs=out_specs, check_vma=False)
```

```python
import functools

import jax
import jax.numpy as jnp
from jax import lax
from jax.experimental import pallas as pl
from jax.experimental.pallas import tpu as pltpu
from jax.sharding import PartitionSpec as P

highest = lax.Precision.HIGHEST
VMEM = pltpu.VMEM
SMEM = pltpu.SMEM


def nt(left, right):
    return lax.dot_general(
        left, right, (((1,), (1,)), ((), ())), precision=highest, preferred_element_type=jnp.float32
    )


def nn(left, right):
    return lax.dot_general(
        left, right, (((1,), (0,)), ((), ())), precision=highest, preferred_element_type=jnp.float32
    )


def tn(left, right):
    return lax.dot_general(
        left, right, (((0,), (0,)), ((), ())), precision=highest, preferred_element_type=jnp.float32
    )


def split_bf16(value):
    high = value.astype(jnp.bfloat16)
    low = (value - high.astype(jnp.float32)).astype(jnp.bfloat16)
    return high, low


def mega_kernel(
    per_col, n_row, n_col, n_panels,
    order_ref, up_len_ref, low_len_ref, tile_ref, *refs,
):
    panel_refs, refs = refs[:n_panels], refs[n_panels:]
    (
        ainv_hbm, parent_ref, up_ref, low_ref, totals_ref,
        whole, spread, gathered, ainv_ref, high_ref, low_part_ref, own, away, mate, line, local,
        terms, landed, totals, tiles, slots,
        a_send, a_recv, c_send, c_recv, g_send, g_recv, l_send, l_recv,
        s_send, s_recv, z_send, z_recv, t_send, t_recv, q_send, q_recv, own_sem, ainv_sem, slot_sem,
    ) = refs
    me_r = lax.axis_index("row")
    me_c = lax.axis_index("col")
    chips = n_col // 2
    z = me_c // 2
    core = me_c % 2
    sibling = me_c + 1 - 2 * core
    combos = 2 * per_col
    parts = n_row // combos
    mine = panel_refs[0].shape[1]
    col_blocks, row_blocks, width, _ = high_ref.shape
    col_live = gathered.shape[2]
    row_live = local.shape[1]

    def remote(src, dst, send, recv, target):
        return pltpu.make_async_remote_copy(
            src_ref=src, dst_ref=dst, send_sem=send, recv_sem=recv,
            device_id=target, device_id_type=pl.DeviceIdType.MESH,
        )

    barrier = pltpu.get_barrier_semaphore()
    for d in range(1, n_row):
        pl.semaphore_signal(barrier, inc=1, device_id={"row": (me_r + d) % n_row},
                            device_id_type=pl.DeviceIdType.MESH)
    for d in range(1, n_col):
        pl.semaphore_signal(barrier, inc=1, device_id={"col": (me_c + d) % n_col},
                            device_id_type=pl.DeviceIdType.MESH)
    pl.semaphore_wait(barrier, n_row + n_col - 2)

    def held(peer):
        if n_panels == 1:
            return panel_refs[0].at[peer]
        return panel_refs[peer // per_col].at[peer % per_col]

    def share(peer, source):
        return remote(held(peer), whole.at[pl.ds(source * mine, mine)],
                      a_send.at[peer], a_recv.at[source], {"row": peer})

    def keep(peer):
        return pltpu.make_async_copy(held(peer), whole.at[pl.ds(me_r * mine, mine)], own_sem)

    def each_peer(act):
        for peer in range(n_row):
            @pl.when(peer != me_r)
            def _():
                act(share(peer, me_r))

    def slot_copy(c, source):
        return remote(tile_ref, tiles.at[source], q_send.at[c], q_recv.at[source], {"col": c})

    each_peer(lambda copy: copy.start())
    for peer in range(n_row):
        @pl.when(peer == me_r)
        def _():
            keep(peer).start()
    fetch = pltpu.make_async_copy(ainv_hbm, ainv_ref, ainv_sem)
    fetch.start()
    for d in range(1, n_col):
        slot_copy((me_c + d) % n_col, me_c).start()
    tiles[me_c] = tile_ref[...]
    fetch.wait()
    for cb in range(col_blocks):
        for rb in range(row_blocks):
            block = ainv_ref[rb * width:(rb + 1) * width, cb * width:(cb + 1) * width]
            high, low = split_bf16(block)
            high_ref[cb, rb] = high
            low_part_ref[cb, rb] = low
    keep(0).wait()
    for d in range(1, n_row):
        share(0, (me_r + d) % n_row).wait_recv()

    my_combo = me_r // parts
    my_node = my_combo % per_col
    my_len = jnp.where(my_combo < per_col, up_len_ref[my_node], low_len_ref[my_node])

    def pick(c):
        for s in range(col_live):
            place = c * col_live + s
            listed_at = order_ref[my_node, place]
            spread[place] = jnp.where(listed_at < my_len, whole[listed_at], 0.0).T

    def ship(c, source):
        return remote(spread.at[pl.ds(c * col_live, col_live)], gathered.at[me_r, source],
                      c_send.at[c], c_recv.at[source], {"col": c})

    def pick_and_ship(c):
        pick(c)
        ship(c, me_c).start()

    def side_chip(t, side):
        chip = (1 - side) * (chips - 1 - t) + side * t
        active = jnp.where(side == 0, chip > z, chip < z)
        return chip, active

    pick(me_c)
    gathered[me_r, me_c] = spread[pl.ds(me_c * col_live, col_live)]

    def ship_step(i, carry):
        chip, active = side_chip(i // 2, i % 2)

        @pl.when(active)
        def _():
            pick_and_ship(2 * chip + core)
            pick_and_ship(2 * chip + 1 - core)

        return carry

    lax.fori_loop(0, 2 * chips, ship_step, 0)
    pick_and_ship(sibling)

    def pass_on(c, peer, source):
        return remote(gathered.at[source, c], gathered.at[source, c],
                      g_send.at[peer, c], g_recv.at[source, c], {"row": peer})

    def forward(c):
        for d in range(1, n_row):
            pass_on(c, (me_r + d) % n_row, me_r).start()

    forward(me_c)
    ship(me_c, sibling).wait_recv()
    forward(sibling)

    def forward_side(i, carry):
        chip, active = side_chip(i // 2, i % 2)

        @pl.when(active)
        def _():
            for c in (2 * chip + core, 2 * chip + 1 - core):
                ship(me_c, c).wait_recv()
                forward(c)

        return carry

    lax.fori_loop(0, 4, forward_side, 0)

    def local_copy(peer, source):
        return remote(spread.at[pl.ds(peer * row_live, row_live)], local.at[source],
                      l_send.at[peer], l_recv.at[source], {"row": peer})

    for d in range(1, n_row):
        local_copy((me_r + d) % n_row, me_r).start()
    local[me_r] = spread[pl.ds(me_r * row_live, row_live)]

    for d in range(1, n_col):
        slot_copy(me_c, (me_c + d) % n_col).wait_recv()
    to_scalars = pltpu.make_async_copy(tiles, slots, slot_sem)
    to_scalars.start()
    to_scalars.wait()

    def product(c, chip, out, send=None):
        for d in range(1, n_row):
            pass_on(c, me_r, (me_r + d) % n_row).wait_recv()
        for node in range(per_col):
            rows = []
            for panel in range(2):
                for part in range(parts):
                    source = (panel * per_col + node) * parts + part
                    rows.append(jnp.concatenate([gathered[source, c, s] for s in range(col_live)], axis=1))
            left_high, left_low = split_bf16(jnp.concatenate(rows, axis=0))
            left_all = jnp.concatenate([left_high, left_high, left_low], axis=1)
            cols = [lax.rem(slots[c, node, me_c * col_live + s], col_blocks) for s in range(col_live)]
            for rb in range(row_live):
                row = lax.rem(slots[c, node, me_r * row_live + rb], row_blocks)
                high = [high_ref[cb, row] for cb in cols]
                low = [low_part_ref[cb, row] for cb in cols]
                right = jnp.concatenate(high + low + high, axis=1)
                total = lax.dot_general(
                    left_all, right, (((1,), (1,)), ((), ())), preferred_element_type=jnp.float32
                )
                for panel in range(2):
                    out[chip, panel * per_col + node, :, rb * width:(rb + 1) * width] = (
                        -total[panel * width:(panel + 1) * width]
                    )
            if send is not None:
                for panel in range(2):
                    send(chip, panel * per_col + node).start()

    def to_mate(chip, s):
        return remote(away.at[chip, s], mate.at[chip, s], s_send.at[chip, s], s_recv.at[chip, s],
                      {"col": sibling})

    def both_products(chip):
        product(2 * chip + 1 - core, chip, away, to_mate)
        product(2 * chip + core, chip, own)

    def onward(chip, s, side):
        slot = jnp.where((side == 1) & (z - 1 == chip), chips, chip)
        return remote(own.at[chip, s], line.at[slot, s], z_send.at[chip, s], z_recv.at[slot, s],
                      {"col": me_c + 2 - 4 * side})

    def arrived(slot, s):
        remote(own.at[0, s], line.at[slot, s], z_send.at[0, s], z_recv.at[slot, s],
               {"col": sibling}).wait_recv()

    def chunk_step(t, carry):
        def compute_side(side, inner):
            chip, active = side_chip(t, side)

            @pl.when(active)
            def _():
                both_products(chip)

            return inner

        def send_side(i, inner):
            s = i // 2
            side = i % 2
            chip, active = side_chip(t, side)

            @pl.when(active)
            def _():
                to_mate(chip, s).wait_recv()
                own[chip, s] = own[chip, s] + mate[chip, s]

                @pl.when(jnp.where(side == 0, z > 0, z < chips - 1))
                def _():
                    arrived(chip, s)
                    own[chip, s] = own[chip, s] + line[chip, s]

                onward(chip, s, side).start()

            return inner

        lax.fori_loop(0, 2, compute_side, 0)
        lax.fori_loop(0, 2 * combos, send_side, 0)
        lax.fori_loop(2 * t + 4, 2 * t + 6, forward_side, 0)
        return carry

    lax.fori_loop(0, chips, chunk_step, 0)
    both_products(z)

    def last_step(s, carry):
        to_mate(z, s).wait_recv()
        own[z, s] = own[z, s] + mate[z, s]

        @pl.when(z > 0)
        def _():
            arrived(z, s)
            own[z, s] = own[z, s] + line[z, s]

        @pl.when(z < chips - 1)
        def _():
            arrived(chips, s)
            own[z, s] = own[z, s] + line[chips, s]

        return carry

    each_peer(lambda copy: copy.wait_send())
    for d in range(1, n_col):
        ship((me_c + d) % n_col, me_c).wait_send()
        slot_copy((me_c + d) % n_col, me_c).wait_send()
    for d in range(1, n_row):
        local_copy((me_r + d) % n_row, me_r).wait_send()
        for c in range(n_col):
            pass_on(c, (me_r + d) % n_row, me_r).wait_send()
    for chip in range(chips):
        for s in range(combos):
            to_mate(chip, s).wait_send()

    part_rows = width // n_row
    rounds = ((0, 2 * per_col),) + tuple((2 * per_col + node, 1) for node in range(per_col))
    n_rounds = len(rounds)

    def full(combo, place):
        return jnp.concatenate([local[combo * parts + part, place] for part in range(parts)], axis=0)

    def spans():
        return [(place, slice(place * width, (place + 1) * width)) for place in range(row_live)]

    def live(node, place, length_ref):
        return order_ref[node, me_r * row_live + place] < length_ref[node]

    def put(kind, node, value):
        for j in range(n_row):
            terms[j, kind * per_col + node] = value[j * part_rows:(j + 1) * part_rows]

    def scatter(at, peer, source):
        part = pl.ds(*rounds[at])
        return remote(terms.at[peer, part], landed.at[source, part], t_send.at[at, peer],
                      t_recv.at[at, source], {"row": peer})

    def spread_total(at, peer, source):
        part = pl.ds(*rounds[at])
        return remote(totals.at[source, part], totals.at[source, part], t_send.at[n_rounds + at, peer],
                      t_recv.at[n_rounds + at, source], {"row": peer})

    def start_round(at):
        for d in range(1, n_row):
            scatter(at, (me_r + d) % n_row, me_r).start()
        part = pl.ds(*rounds[at])
        landed[me_r, part] = terms[me_r, part]

    def sum_round(at):
        for d in range(1, n_row):
            scatter(at, me_r, (me_r + d) % n_row).wait_recv()
        part = pl.ds(*rounds[at])
        total = landed[0, part]
        for j in range(1, n_row):
            total = total + landed[j, part]
        totals[me_r, part] = total
        for d in range(1, n_row):
            spread_total(at, (me_r + d) % n_row, me_r).start()

    for d in range(1, n_row):
        local_copy(me_r, (me_r + d) % n_row).wait_recv()
    lax.fori_loop(0, per_col, last_step, 0)
    for node in range(per_col):
        upper_term = jnp.zeros((width, width), jnp.float32)
        cross_term = jnp.zeros((width, width), jnp.float32)
        for place, span in spans():
            upper = jnp.where(live(node, place, up_len_ref), own[z, node, :, span], 0.0)
            up_ref[node, :, span] = upper
            upper_term = upper_term + nt(full(node, place), upper)
            cross_term = cross_term + nt(upper, full(per_col + node, place))
        put(0, node, upper_term)
        put(1, node, cross_term)
    start_round(0)
    for node in range(per_col):
        low_ref[node] = tn(parent_ref[node], up_ref[node])
    for node in range(per_col):
        last_step(per_col + node, 0)
        lower_term = jnp.zeros((width, width), jnp.float32)
        for place, span in spans():
            lower = own[z, per_col + node, :, span] - low_ref[node, :, span]
            lower = jnp.where(live(node, place, low_len_ref), lower, 0.0)
            low_ref[node, :, span] = lower
            lower_term = lower_term + nt(full(per_col + node, place), lower)
        put(2, node, lower_term)
        start_round(1 + node)
        sum_round(node)
    sum_round(per_col)
    for at in range(n_rounds):
        for d in range(1, n_row):
            spread_total(at, me_r, (me_r + d) % n_row).wait_recv()
    totals_ref[...] = totals[...]

    for d in range(1, n_row):
        for at in range(n_rounds):
            scatter(at, (me_r + d) % n_row, me_r).wait_send()
            spread_total(at, (me_r + d) % n_row, me_r).wait_send()

    def drain(i, carry):
        chip = i // combos

        @pl.when(chip != z)
        def _():
            onward(chip, i % combos, jnp.where(chip > z, 0, 1)).wait_send()

        return carry

    lax.fori_loop(0, chips * combos, drain, 0)


def write_kernel(row_blocks, slot_ref, up_ref, low_ref, totals_ref, parent_ref, updinv_ref, lowdinv_ref,
                 up_off_ref, up_diag_ref, low_off_ref, prow_ref, low_diag_ref):
    per_col, width, _ = parent_ref.shape
    n_row = totals_ref.shape[0]
    row_live = up_ref.shape[2] // width
    up_off_ref[...] = jnp.zeros_like(up_off_ref)
    low_off_ref[...] = jnp.zeros_like(low_off_ref)

    def summed(kind, node):
        return jnp.concatenate([totals_ref[j, kind * per_col + node] for j in range(n_row)], axis=0)

    for node in range(per_col):
        for place in range(row_live):
            span = slice(place * width, (place + 1) * width)
            block = lax.rem(slot_ref[node, lax.axis_index("row") * row_live + place], row_blocks)
            at = pl.ds(pl.multiple_of(block * width, width), width)
            up_off_ref[node, :, at] = up_ref[node, :, span]
            low_off_ref[node, :, at] = low_ref[node, :, span]
        parent = parent_ref[node]
        diag_up = updinv_ref[node] - summed(0, node)
        prow = -(nn(diag_up, parent) + summed(1, node))
        up_diag_ref[node] = diag_up
        prow_ref[node] = prow
        low_diag_ref[node] = lowdinv_ref[node] - tn(parent, prow) - summed(2, node)


def body(
    n_row,
    n_col,
    ainv_top,
    block_owner,
    upper_list,
    upper_len,
    upper_panel,
    upper_dinv,
    lower_len,
    lower_panel,
    lower_parent,
    lower_dinv,
):
    width = upper_dinv.shape[-1]
    per_col = upper_dinv.shape[0]
    local_rows, local_cols = ainv_top.shape
    row_blocks = local_rows // width
    col_blocks = local_cols // width
    row_live = row_blocks // 2
    col_live = col_blocks // 2
    total = block_owner.shape[0]
    listed = upper_list.shape[1]
    mine = listed // n_row
    combos = 2 * per_col
    parts = n_row // combos
    piece = width // parts

    every = jnp.arange(total, dtype=jnp.int32)
    places = jnp.arange(listed, dtype=jnp.int32)
    slots = jnp.sum(
        jnp.where(upper_list[:, :, None] == every, block_owner[None, None, :], 0), axis=2
    )
    rank = jnp.sum((slots[:, None, :] < slots[:, :, None]).astype(jnp.int32), axis=2)
    hit = rank[:, :, None] == places[None, None, :]
    order = jnp.sum(jnp.where(hit, places[None, :, None], 0), axis=1)
    sorted_slots = jnp.sum(jnp.where(hit, slots[:, :, None], 0), axis=1)
    tile = jnp.pad(sorted_slots, ((0, 8 - per_col), (0, 128 - listed)))

    if parts == 1:
        panels = tuple(panel.reshape(per_col, mine, width, width) for panel in (upper_panel, lower_panel))
    else:
        both = jnp.concatenate([upper_panel, lower_panel], axis=0)
        both = both.reshape(combos, mine, width, parts, piece)
        panels = (both.transpose(0, 3, 1, 2, 4).reshape(n_row, mine, width, piece),)
    chips = n_col // 2
    live_width = row_live * width
    f32 = jnp.float32
    dma = pltpu.SemaphoreType.DMA
    square = jax.ShapeDtypeStruct((per_col, width, width), f32)
    wide = jax.ShapeDtypeStruct((per_col, width, local_rows), f32)
    chunks = VMEM((chips, combos, width, live_width), f32)
    shares = VMEM((n_row, 3 * per_col, width // n_row, width), f32)
    rows = jax.ShapeDtypeStruct((per_col, width, live_width), f32)
    upper_rows, lower_rows, totals = pl.pallas_call(
        functools.partial(mega_kernel, per_col, n_row, n_col, len(panels)),
        out_shape=(rows, rows, jax.ShapeDtypeStruct((n_row, 3 * per_col, width // n_row, width), f32)),
        in_specs=(
            [pl.BlockSpec(memory_space=SMEM)] * 3
            + [pl.BlockSpec(memory_space=VMEM)]
            + [pl.BlockSpec(memory_space=pl.ANY)] * (len(panels) + 1)
            + [pl.BlockSpec(memory_space=VMEM)]
        ),
        out_specs=(pl.BlockSpec(memory_space=VMEM),) * 3,
        scratch_shapes=[
            VMEM((listed, width, piece), f32),
            VMEM((listed, piece, width), f32),
            VMEM((n_row, n_col, col_live, piece, width), f32),
            VMEM((local_rows, local_cols), f32),
            VMEM((col_blocks, row_blocks, width, width), jnp.bfloat16),
            VMEM((col_blocks, row_blocks, width, width), jnp.bfloat16),
            chunks,
            chunks,
            chunks,
            VMEM((chips + 1, combos, width, live_width), f32),
            VMEM((n_row, row_live, piece, width), f32),
            shares,
            shares,
            shares,
            VMEM((n_col, 8, 128), jnp.int32),
            SMEM((n_col, 8, 128), jnp.int32),
            dma((n_row,)),
            dma((n_row,)),
            dma((n_col,)),
            dma((n_col,)),
            dma((n_row, n_col)),
            dma((n_row, n_col)),
            dma((n_row,)),
            dma((n_row,)),
            dma((chips, combos)),
            dma((chips, combos)),
            dma((chips, combos)),
            dma((chips + 1, combos)),
            dma((2 * (1 + per_col), n_row)),
            dma((2 * (1 + per_col), n_row)),
            dma((n_col,)),
            dma((n_col,)),
            dma(()),
            dma(()),
            dma(()),
        ],
        compiler_params=pltpu.CompilerParams(
            collective_id=0, has_side_effects=True, vmem_limit_bytes=60 * 1024 * 1024
        ),
        name="selected_inverse",
    )(order, upper_len, lower_len, tile, *panels, ainv_top, lower_parent)
    return pl.pallas_call(
        functools.partial(write_kernel, row_blocks),
        out_shape=(wide, square, wide, square, square),
        in_specs=[pl.BlockSpec(memory_space=SMEM)] + [pl.BlockSpec(memory_space=VMEM)] * 6,
        out_specs=(pl.BlockSpec(memory_space=VMEM),) * 5,
        compiler_params=pltpu.CompilerParams(vmem_limit_bytes=60 * 1024 * 1024),
        name="write_out",
    )(sorted_slots, upper_rows, lower_rows, totals, lower_parent, upper_dinv, lower_dinv)


def solution(mesh):
    in_specs = (
        P("row", "col"),
        P(),
        P("col", None),
        P("col"),
        P("col", "row", None),
        P("col", None, None),
        P("col"),
        P("col", "row", None),
        P("col", None, None),
        P("col", None, None),
    )
    out_specs = (
        P("col", None, "row"),
        P("col", None, None),
        P("col", None, "row"),
        P("col", None, None),
        P("col", None, None),
    )
    inner = functools.partial(body, mesh.shape["row"], mesh.shape["col"])
    return jax.shard_map(inner, mesh=mesh, in_specs=in_specs, out_specs=out_specs, check_vma=False)
```
